32 devices in a mesh: seq: 8 (over z, x), dp: 4 (over y, core).
Axes of the slice: x: 2, y: 2, z: 4, core: 2. Of those that a mesh axis runs over, the one named last changes fastest.
Arguments:
- activations: bfloat16 [4, 2048, 8192], P('dp', 'seq'), may hold values from -16 to 16
- query_states: bfloat16 [4, 2048, 4096], P('dp', 'seq'), may hold values from -400 to 400
- key_states: bfloat16 [4, 2048, 512], P('dp', 'seq'), may hold values from -6 to 6
- value_states: bfloat16 [4, 2048, 512], P('dp', 'seq'), may hold values from -6 to 6
- output_grad: bfloat16 [4, 2048, 4096], P('dp', 'seq'), may hold values from -6.5 to 6.5
- query_lowrank: bfloat16 [4, 2048, 16], P('dp', 'seq'), may hold values from -6 to 6
- value_lowrank: bfloat16 [4, 2048, 16], P('dp', 'seq'), may hold values from -6 to 6
- query_up_matrix: bfloat16 [16, 4096], replicated, may hold values from -0.09375 to 0.09375
- value_up_matrix: bfloat16 [16, 512], replicated, may hold values from -0.25 to 0.25
- noise_query_down: float32 [8192, 16], P('seq'), may hold values from -6 to 6
- noise_query_lift: float32 [16, 4096], P(None, 'seq'), may hold values from -6 to 6
- noise_value_down: float32 [8192, 16], P('seq'), may hold values from -6 to 6
- noise_value_lift: float32 [16, 512], P(None, 'seq'), may hold values from -6 to 6
- block_order: int32 [4, 8], P('dp', 'seq'), may hold values from 0 to 7, as said below
- valid_lengths: int32 [4], P('dp'), may hold values from 512 to 2048, as said below
Outputs:
- example_norms: float32 [4], P('dp')
- query_down_sum: float32 [8192, 16], P('seq')
- query_lift_sum: float32 [16, 4096], P(None, 'seq')
- value_down_sum: float32 [8192, 16], P('seq')
- value_lift_sum: float32 [16, 512], P(None, 'seq')
The draws below stay inside these ranges and needn't reach their ends.
Inputs may be any that keep to these rules, and one draw needn't show every extreme that they name: `valid_lengths`: some example has all 2048 tokens valid in every draw. Each example's stored blocks hold the sequence blocks in cyclic order: block_order[b, j] = (s_b + j) mod 8, with a starting block s_b from 1 to 7.
All inputs are finite; a program needn't handle non-finite values.
Results may differ from the reference program's by a relative error of at most 0.0073.
Values may be sent and summed in bfloat16 or wider, within the bound.
A program may use at most 64 MiB of HBM per device.

```python
import math
import jax
import jax.numpy as jnp
from jax import lax

D = 8192
HEAD_SIZE = 128
RANK = 16
TOK = 256
QUERY_WIDTH = 4096
KVW = 512
SEQUENCE_BLOCKS = 8
SEQ = 2048
EXAMPLE_COUNT = 4
PCOUNT = 335872


def block_pairing(key):
    return jax.random.permutation(key, SEQUENCE_BLOCKS)


def draw_activations(key, part):
    key = jax.random.fold_in(key, 17)
    key_base, key_mode, key_pair = jax.random.split(key, 3)
    width_block = D // SEQUENCE_BLOCKS
    shape = (EXAMPLE_COUNT, SEQUENCE_BLOCKS, TOK, SEQUENCE_BLOCKS, width_block)
    base = jnp.clip(jax.random.normal(key_base, shape, jnp.float32), -5.0, 5.0)
    pairing = jax.vmap(block_pairing)(jax.random.split(key_pair, EXAMPLE_COUNT))
    column_blocks = jnp.arange(SEQUENCE_BLOCKS)
    paired = pairing[:, :, None] == column_blocks[None, None, :]
    spike = jnp.where(paired, 3.0, 1.0)[:, :, None, :, None]
    mode = jnp.clip(jax.random.normal(key_mode, (EXAMPLE_COUNT, 1, 1, SEQUENCE_BLOCKS, width_block), jnp.float32), -4.0, 4.0)
    rows = base * spike + 0.22 / math.sqrt(TOK) * mode
    return rows.reshape(EXAMPLE_COUNT, SEQ, D).astype(jnp.bfloat16)


def draw_output_grad(key, part):
    key = jax.random.fold_in(key, 19)
    key_base, key_mode = jax.random.split(key)
    shape = (EXAMPLE_COUNT, SEQ, QUERY_WIDTH)
    base = jnp.clip(jax.random.normal(key_base, shape, jnp.float32), -6.0, 6.0)
    mode = jnp.clip(jax.random.normal(key_mode, (EXAMPLE_COUNT, 1, QUERY_WIDTH), jnp.float32), -4.0, 4.0)
    rows = 0.995 * base + 0.1 * mode
    return rows.astype(jnp.bfloat16)


def draw_query_states(key, part):
    key = jax.random.fold_in(key, 11)
    rows = jnp.clip(jax.random.normal(key, (EXAMPLE_COUNT, SEQ, QUERY_WIDTH), jnp.float32), -6.0, 6.0)
    return rows.astype(jnp.bfloat16)


def draw_key_states(key, part):
    key = jax.random.fold_in(key, 13)
    rows = jnp.clip(jax.random.normal(key, (EXAMPLE_COUNT, SEQ, KVW), jnp.float32), -6.0, 6.0)
    return rows.astype(jnp.bfloat16)


def draw_block_order(key, part):
    key = jax.random.fold_in(key, 7)
    starts = jax.random.randint(key, (EXAMPLE_COUNT,), 1, SEQUENCE_BLOCKS)
    stored = jnp.arange(SEQUENCE_BLOCKS, dtype=jnp.int32)
    return ((starts[:, None] + stored[None, :]) % SEQUENCE_BLOCKS).astype(jnp.int32)


def draw_valid_lengths(key, part):
    key = jax.random.fold_in(key, 5)
    first, second = jax.random.split(key)
    drawn = jax.random.randint(first, (EXAMPLE_COUNT,), SEQ // 4, SEQ + 1)
    chosen = jax.random.randint(second, (), 0, EXAMPLE_COUNT)
    return jnp.where(jnp.arange(EXAMPLE_COUNT) == chosen, SEQ, drawn).astype(jnp.int32)


def block_scale(own_key, dims, cuts, least, top_value):
    level, own = 1.0, jax.random.fold_in(own_key, 6)
    for position, blocks in cuts:
        steps = jnp.exp(jax.random.uniform(jax.random.fold_in(own, position), (blocks,), jnp.float32, least / len(cuts), top_value / len(cuts)))
        level = level * jnp.repeat(steps, dims[position] // blocks).reshape([-1 if axis == position else 1 for axis in range(len(dims))])
    return level


def scatter_about(own_key, extent, scale, bound, cuts=(), held_as=jnp.bfloat16):
    level = block_scale(own_key, extent, cuts, -0.22, 0.18) if cuts else 1.0
    array = jax.random.normal(own_key, extent, jnp.float32) * scale * level
    return jnp.minimum(jnp.maximum(array, -bound), bound).astype(held_as)


def setup_inputs(seed: int = 0) -> dict:
    key_of = jax.random.split(jax.random.key(seed), 16)
    return {
        "activations": draw_activations(jax.random.fold_in(key_of[15], 71), 0),
        "query_states": draw_query_states(jax.random.fold_in(key_of[15], 71), 0),
        "key_states": draw_key_states(jax.random.fold_in(key_of[15], 71), 0),
        "value_states": scatter_about(key_of[3], (EXAMPLE_COUNT, SEQ, KVW), 1.0, 6.0, ((0, 4), (1, 8))),
        "output_grad": draw_output_grad(jax.random.fold_in(key_of[15], 71), 0),
        "query_lowrank": scatter_about(key_of[5], (EXAMPLE_COUNT, SEQ, RANK), 1.0, 6.0, ((0, 4), (1, 8))),
        "value_lowrank": scatter_about(key_of[6], (EXAMPLE_COUNT, SEQ, RANK), 1.0, 6.0, ((0, 4), (1, 8))),
        "query_up_matrix": scatter_about(key_of[7], (RANK, QUERY_WIDTH), QUERY_WIDTH ** -0.5, 0.09375),
        "value_up_matrix": scatter_about(key_of[8], (RANK, KVW), KVW ** -0.5, 0.25),
        "noise_query_down": scatter_about(key_of[9], (D, RANK), 1.0, 6.0, ((0, 8),), jnp.float32),
        "noise_query_lift": scatter_about(key_of[10], (RANK, QUERY_WIDTH), 1.0, 6.0, ((1, 8),), jnp.float32),
        "noise_value_down": scatter_about(key_of[11], (D, RANK), 1.0, 6.0, ((0, 8),), jnp.float32),
        "noise_value_lift": scatter_about(key_of[12], (RANK, KVW), 1.0, 6.0, ((1, 8),), jnp.float32),
        "block_order": draw_block_order(jax.random.fold_in(key_of[15], 71), 0),
        "valid_lengths": draw_valid_lengths(jax.random.fold_in(key_of[15], 71), 0),
    }


ADAPTER_SCALE = 2.0
NOISE_STD = 0.5
STABLE = 0.01
ROPE_BASE = 500000.0

def rotate(values, positions, sign):
    row_count = values.shape[0]
    half = HEAD_SIZE // 2
    grid = values.reshape(row_count, -1, HEAD_SIZE)
    freqs = ROPE_BASE ** (-2.0 * jnp.arange(half).astype(jnp.float32) / HEAD_SIZE)
    angle = positions.astype(jnp.float32)[:, None] * freqs[None, :]
    cosine = jnp.cos(angle)[:, None, :]
    sine = sign * jnp.sin(angle)[:, None, :]
    first = grid[..., :half]
    second = grid[..., half:]
    turned = jnp.concatenate([first * cosine - second * sine, first * sine + second * cosine], -1)
    return turned.reshape(row_count, -1)

def window_grads(query_rot, key_rot, value_rows, grad_eff, allowed):
    row_count = query_rot.shape[0]
    key_count = key_rot.shape[0]
    heads_kv = key_rot.shape[1] // HEAD_SIZE
    group = query_rot.shape[1] // key_rot.shape[1]
    scaling = 1.0 / math.sqrt(HEAD_SIZE)
    query_split = jnp.moveaxis(query_rot.reshape(row_count, heads_kv, group, HEAD_SIZE), 1, 0)
    grad_split = jnp.moveaxis(grad_eff.reshape(row_count, heads_kv, group, HEAD_SIZE), 1, 0)
    key_split = jnp.moveaxis(key_rot.reshape(key_count, heads_kv, HEAD_SIZE), 1, 0)
    value_split = jnp.moveaxis(value_rows.reshape(key_count, heads_kv, HEAD_SIZE), 1, 0)

    def one_head(items):
        query_head, grad_head, key_head, value_head = [item.astype(jnp.float32) for item in items]
        scores = jnp.einsum('tgd,kd->gtk', query_head, key_head) * scaling
        scores = jnp.where(allowed[None], scores, -jnp.inf)
        row_max = lax.optimization_barrier(jnp.max(scores, -1, keepdims=True))
        shifted = jnp.exp(scores - row_max)
        probs = shifted / lax.optimization_barrier(jnp.sum(shifted, -1, keepdims=True))
        probs_low = probs.astype(jnp.bfloat16).astype(jnp.float32)
        attended = jnp.einsum('gtk,kd->tgd', probs_low, value_head)
        delta = lax.optimization_barrier(jnp.sum(grad_head * attended, -1))
        dprob = jnp.einsum('tgd,kd->gtk', grad_head, value_head)
        dscore = (probs * (dprob - jnp.transpose(delta)[:, :, None])).astype(jnp.bfloat16).astype(jnp.float32)
        query_gradient = jnp.einsum('gtk,kd->tgd', dscore, key_head) * scaling
        dvalue = jnp.einsum('gtk,tgd->kd', probs_low, grad_head)
        return (query_gradient, dvalue)
    query_gradient, dvalue = lax.map(one_head, (query_split, grad_split, key_split, value_split))
    query_gradient = jnp.moveaxis(query_gradient, 0, 1).reshape(row_count, -1)
    dvalue = jnp.moveaxis(dvalue, 0, 1).reshape(key_count, -1)
    return (query_gradient, dvalue)

def example_grads(items):
    acts, queries, keyrows, valrows, outgrad, query_reduced, value_reduced, order, length, query_up_matrix, value_up_matrix = items
    offsets = jnp.arange(TOK, dtype=jnp.int32)
    positions = (order[:, None] * TOK + offsets[None, :]).reshape(-1).astype(jnp.int32)
    query_rot = rotate(queries.astype(jnp.float32), positions, 1.0).astype(jnp.bfloat16)
    key_rot = rotate(keyrows.astype(jnp.float32), positions, 1.0).astype(jnp.bfloat16)
    keep = positions < length
    grad_eff = jnp.where(keep[:, None], outgrad, jnp.zeros_like(outgrad))

    def per_stored(index):
        before = ((index + SEQUENCE_BLOCKS - 1) % SEQUENCE_BLOCKS).astype(jnp.int32)
        start = (index * TOK).astype(jnp.int32)
        start_before = (before * TOK).astype(jnp.int32)
        query_part = lax.dynamic_slice_in_dim(query_rot, start, TOK, 0)
        grad_part = lax.dynamic_slice_in_dim(grad_eff, start, TOK, 0)
        key_part = jnp.concatenate([lax.dynamic_slice_in_dim(key_rot, start, TOK, 0), lax.dynamic_slice_in_dim(key_rot, start_before, TOK, 0)], 0)
        value_part = jnp.concatenate([lax.dynamic_slice_in_dim(valrows, start, TOK, 0), lax.dynamic_slice_in_dim(valrows, start_before, TOK, 0)], 0)
        query_pos = lax.dynamic_slice_in_dim(positions, start, TOK, 0)
        key_pos = jnp.concatenate([query_pos, lax.dynamic_slice_in_dim(positions, start_before, TOK, 0)], 0)
        allowed = key_pos[None, :] <= query_pos[:, None]
        query_gradient, dvalue = window_grads(query_part, key_part, value_part, grad_part, allowed)
        return (query_gradient, dvalue[:TOK], dvalue[TOK:])
    dquery_all, dvalue_self, dvalue_before = lax.map(per_stored, jnp.arange(SEQUENCE_BLOCKS, dtype=jnp.int32))
    dvalue = (dvalue_self + jnp.roll(dvalue_before, -1, axis=0)).reshape(SEQ, -1)
    query_gradient = rotate(dquery_all.reshape(SEQ, -1), positions, -1.0).astype(jnp.bfloat16)
    value_projected_gradient = dvalue.astype(jnp.bfloat16)
    query_upward_gradient = ADAPTER_SCALE * jnp.dot(query_reduced.T, query_gradient, preferred_element_type=jnp.float32)
    query_reduced_gradient = (ADAPTER_SCALE * jnp.dot(query_gradient, query_up_matrix.T, preferred_element_type=jnp.float32)).astype(jnp.bfloat16)
    grad_query_down = jnp.dot(acts.T, query_reduced_gradient, preferred_element_type=jnp.float32)
    value_upward_gradient = ADAPTER_SCALE * jnp.dot(value_reduced.T, value_projected_gradient, preferred_element_type=jnp.float32)
    value_reduced_gradient = (ADAPTER_SCALE * jnp.dot(value_projected_gradient, value_up_matrix.T, preferred_element_type=jnp.float32)).astype(jnp.bfloat16)
    grad_value_down = jnp.dot(acts.T, value_reduced_gradient, preferred_element_type=jnp.float32)
    return (grad_query_down, query_upward_gradient, grad_value_down, value_upward_gradient)

def reference(activations, query_states, key_states, value_states, output_grad, query_lowrank, value_lowrank, query_up_matrix, value_up_matrix, noise_query_down, noise_query_lift, noise_value_down, noise_value_lift, block_order, valid_lengths):

    def one_example(items):
        return example_grads(items + (query_up_matrix, value_up_matrix))
    grad_qd, grad_ql, grad_vd, grad_vl = lax.map(one_example, (activations, query_states, key_states, value_states, output_grad, query_lowrank, value_lowrank, block_order, valid_lengths))
    squares = lax.optimization_barrier(jnp.sum(grad_qd * grad_qd, (1, 2))) + lax.optimization_barrier(jnp.sum(grad_ql * grad_ql, (1, 2)))
    squares = squares + lax.optimization_barrier(jnp.sum(grad_vd * grad_vd, (1, 2))) + lax.optimization_barrier(jnp.sum(grad_vl * grad_vl, (1, 2)))
    example_norms = jnp.sqrt(squares)
    factor = math.sqrt(PCOUNT) / (example_norms + STABLE)
    query_down_sum = lax.optimization_barrier(jnp.sum(factor[:, None, None] * grad_qd, 0)) + NOISE_STD * noise_query_down
    query_lift_sum = lax.optimization_barrier(jnp.sum(factor[:, None, None] * grad_ql, 0)) + NOISE_STD * noise_query_lift
    value_down_sum = lax.optimization_barrier(jnp.sum(factor[:, None, None] * grad_vd, 0)) + NOISE_STD * noise_value_down
    value_lift_sum = lax.optimization_barrier(jnp.sum(factor[:, None, None] * grad_vl, 0)) + NOISE_STD * noise_value_lift
    return (example_norms, query_down_sum, query_lift_sum, value_down_sum, value_lift_sum)
```

```python
import functools
import math

import jax
import jax.numpy as jnp
from jax import lax
from jax.experimental import pallas as pl
from jax.experimental.pallas import tpu as pltpu
from jax.sharding import PartitionSpec as P

HEAD = 128
PCOUNT = 335872
ADAPTER_SCALE = 2.0
NOISE_STD = 0.5
STABLE = 0.01
ROPE_BASE = 500000.0
NEG = -1e30
F32 = jnp.float32
BF16 = jnp.bfloat16
MESH = pl.DeviceIdType.MESH


def dot(a, b):
    return jnp.dot(a, b, preferred_element_type=F32)


def dot_nt(a, b):
    return lax.dot_general(a, b, (((1,), (1,)), ((), ())), preferred_element_type=F32)


def lane_piece(x, j, width):
    if width >= HEAD:
        return x
    if j:
        x = pltpu.roll(x, HEAD - j * width, 1)
    lanes = lax.broadcasted_iota(jnp.int32, x.shape, 1)
    return jnp.where(lanes < width, x, 0.0)


def kernel(
    n,
    m,
    order_ref,
    valid_ref,
    q_hbm,
    g_hbm,
    acts_hbm,
    k_ref,
    v_ref,
    cos_ref,
    sin_ref,
    qlt_ref,
    vlt_ref,
    qup_ref,
    vup_ref,
    nqd_ref,
    nql_ref,
    nvd_ref,
    nvl_ref,
    norm_ref,
    oqd_ref,
    oql_ref,
    ovd_ref,
    ovl_ref,
    q_scr,
    g_scr,
    acts_scr,
    kwin,
    vwin,
    vlt_prev,
    kt_scr,
    cost_scr,
    sint_scr,
    dv_scr,
    dlq_scr,
    dlv_scr,
    ret_send,
    ret_recv,
    send_d,
    recv_d,
    send_l,
    recv_l,
    acc_d,
    acc_l,
    share_d,
    share_l,
    peer_d,
    peer_l,
    sq_send,
    sq_recv,
    fac_send,
    fac_recv,
    local_sem,
    halo_ssem,
    halo_rsem,
    ret_ssem,
    ret_rsem,
    l_ssem,
    l_rsem,
    dq_ssem,
    dq_rsem,
    dv_ssem,
    dv_rsem,
    sq_ssem,
    sq_rsem,
    shd_ssem,
    shd_rsem,
    shl_ssem,
    shl_rsem,
    fac_ssem,
    fac_rsem,
):
    me = lax.axis_index("seq")
    ex = lax.axis_index("dp")
    right = lax.rem(me + 1, n)
    left = lax.rem(me + n - 1, n)
    tok = k_ref.shape[0]
    groups = k_ref.shape[1] // HEAD
    heads = q_scr.shape[1] // (groups * HEAD)
    wd = acts_scr.shape[1] // n
    wq = q_scr.shape[1] // n
    wqp = max(wq, HEAD)
    wv = k_ref.shape[1] // n
    scaling = 1.0 / math.sqrt(HEAD)
    c2 = scaling * math.log2(math.e)

    load_q = pltpu.make_async_copy(q_hbm, q_scr, local_sem.at[0])
    load_g = pltpu.make_async_copy(g_hbm, g_scr, local_sem.at[1])
    load_acts = pltpu.make_async_copy(acts_hbm, acts_scr, local_sem.at[2])
    load_q.start()
    load_g.start()
    load_acts.start()

    barrier = pltpu.get_barrier_semaphore()

    def greet_seq(k, _):
        peer = lax.rem(me + k, n)
        pl.semaphore_signal(barrier, inc=1, device_id={"seq": peer}, device_id_type=MESH)
        return 0

    lax.fori_loop(1, n, greet_seq, 0)
    for k in range(1, m):
        peer = lax.rem(ex + k, m)
        pl.semaphore_signal(barrier, inc=1, device_id={"dp": peer}, device_id_type=MESH)

    cos = cos_ref[...]
    sin = sin_ref[...]
    for c in range(groups):
        cols = slice(c * HEAD, (c + 1) * HEAD)
        k = k_ref[:, cols].astype(F32)
        kr = k * cos + pltpu.roll(k, HEAD // 2, 1) * sin
        kwin[0:tok, cols] = kr.astype(BF16)
        kt_scr[cols, 0:tok] = kr.T.astype(BF16)
    pl.semaphore_wait(barrier, n - 1 + m - 1)

    def halo(i, src, dst):
        return pltpu.make_async_remote_copy(
            src_ref=src,
            dst_ref=dst,
            send_sem=halo_ssem.at[i],
            recv_sem=halo_rsem.at[i],
            device_id={"seq": right},
            device_id_type=MESH,
        )

    halos = [
        halo(0, kwin.at[pl.ds(0, tok)], kwin.at[pl.ds(tok, tok)]),
        halo(1, v_ref, vwin.at[pl.ds(tok, tok)]),
        halo(2, vlt_ref, vlt_prev),
    ]
    for h in halos:
        h.start()
    vwin[0:tok, :] = v_ref[...]
    cost_scr[...] = cos.T
    sint_scr[...] = sin.T
    send_l[...] = jnp.zeros_like(send_l)
    dlq_scr[...] = jnp.zeros_like(dlq_scr)
    dlv_scr[...] = jnp.zeros_like(dlv_scr)

    order = order_ref[0, 0]
    valid = valid_ref[0]
    rows = lax.broadcasted_iota(jnp.int32, (tok, HEAD), 0) + order * tok
    keep = jnp.where(rows < valid, 1.0, 0.0).astype(BF16)
    bias = jnp.where(order > 0, 0.0, NEG).astype(F32)

    load_q.wait()

    def rope_queries(h, _):
        cols = pl.ds(pl.multiple_of(h * HEAD, HEAD), HEAD)
        q = q_scr[:, cols].astype(F32)
        q_scr[:, cols] = (q * cos_ref[...] + pltpu.roll(q, HEAD // 2, 1) * sin_ref[...]).astype(BF16)
        return 0

    lax.fori_loop(0, groups * heads, rope_queries, 0, unroll=4)
    load_g.wait()
    for h in halos:
        h.wait()
    for c in range(groups):
        cols = slice(c * HEAD, (c + 1) * HEAD)
        kt_scr[cols, tok : 2 * tok] = kwin[tok : 2 * tok, cols].astype(F32).T.astype(BF16)

    key_at = lax.broadcasted_iota(jnp.int32, (tok, tok), 0)
    row_at = lax.broadcasted_iota(jnp.int32, (tok, tok), 1)
    causal = key_at <= row_at

    def one_head(c, i):
        h = c * heads + i
        kcols = pl.ds(pl.multiple_of(c * HEAD, HEAD), HEAD)
        cols = pl.ds(pl.multiple_of(h * HEAD, HEAD), HEAD)
        qr = q_scr[:, cols]
        g = g_scr[:, cols] * keep
        s = dot_nt(kwin[:, kcols], qr)
        own = jnp.where(causal, s[:tok], NEG)
        prev = s[tok:]
        top = jnp.maximum(
            jnp.max(own, 0, keepdims=True), jnp.max(prev, 0, keepdims=True) + bias
        )
        shift = top * c2
        e_own = jnp.exp2(own * c2 - shift)
        e_prev = jnp.exp2(prev * c2 - (shift - bias))
        total = jnp.sum(e_own, 0, keepdims=True) + jnp.sum(e_prev, 0, keepdims=True)
        p = jnp.concatenate([e_own, e_prev], 0) * (1.0 / total)
        dp = dot_nt(vwin[:, kcols], g)
        delta = jnp.sum(p * dp, 0, keepdims=True)
        ds = (p * (dp - delta)).astype(BF16)
        dv = dot(p.astype(BF16), g)
        dq = dot(kt_scr[kcols, :], ds) * scaling
        half = HEAD // 2
        swapped = jnp.concatenate([dq[half:], dq[:half]], 0)
        dq_low = (dq * cost_scr[...] - swapped * sint_scr[...]).astype(BF16)
        lift = ADAPTER_SCALE * dot_nt(qlt_ref[...], dq_low)
        dlq = dot(qup_ref[:, cols], dq_low)
        if wq >= HEAD:
            slot = h * HEAD // wq
            at = pl.multiple_of(lax.rem(h * HEAD, wq), HEAD)
            send_l[slot, :, pl.ds(at, HEAD)] = lift.astype(BF16)
        else:
            per = HEAD // wq
            for j in range(per):
                send_l[h * per + j, :, 0:HEAD] = lane_piece(lift, j, wq).astype(BF16)
        return dv, dlq

    unroll = 4

    def one_group(c, _):
        dv_scr[...] = jnp.zeros_like(dv_scr)

        def some_heads(step, _):
            dvs = None
            dlqs = None
            for u in range(unroll):
                dv, dlq = one_head(c, step * unroll + u)
                dvs = dv if dvs is None else dvs + dv
                dlqs = dlq if dlqs is None else dlqs + dlq
            dv_scr[...] += dvs
            dlq_scr[...] += dlqs
            return 0

        lax.fori_loop(0, heads // unroll, some_heads, 0)
        kcols = pl.ds(pl.multiple_of(c * HEAD, HEAD), HEAD)
        dv_low = dv_scr[...].astype(BF16)
        vup = vup_ref[:, kcols]
        dlv_scr[...] += dot_nt(vup, dv_low)
        vlift = ADAPTER_SCALE * (dot(vlt_ref[...], dv_low[:tok]) + dot(vlt_prev[...], dv_low[tok:]))
        per = HEAD // wv
        for j in range(per):
            send_l[c * per + j, :, wqp : wqp + HEAD] = lane_piece(vlift, j, wv).astype(BF16)
        return 0

    lax.fori_loop(0, groups, one_group, 0)

    ret_send[...] = dlv_scr[:, tok : 2 * tok]
    ret = pltpu.make_async_remote_copy(
        src_ref=ret_send,
        dst_ref=ret_recv,
        send_sem=ret_ssem,
        recv_sem=ret_rsem,
        device_id={"seq": left},
        device_id_type=MESH,
    )
    ret.start()

    def to_seq(src, dst, ssem, rsem, peer, slot):
        return pltpu.make_async_remote_copy(
            src_ref=src,
            dst_ref=dst,
            send_sem=ssem.at[peer],
            recv_sem=rsem.at[slot],
            device_id={"seq": peer},
            device_id_type=MESH,
        )

    def lift_copy(peer, slot):
        return to_seq(send_l.at[peer], recv_l.at[slot], l_ssem, l_rsem, peer, slot)

    half_rows = qlt_ref.shape[0]

    def query_copy(peer, slot):
        return to_seq(
            send_d.at[peer, pl.ds(0, half_rows)],
            recv_d.at[slot, pl.ds(0, half_rows)],
            dq_ssem,
            dq_rsem,
            peer,
            slot,
        )

    def value_copy(peer, slot):
        return to_seq(
            send_d.at[peer, pl.ds(half_rows, half_rows)],
            recv_d.at[slot, pl.ds(half_rows, half_rows)],
            dv_ssem,
            dv_rsem,
            peer,
            slot,
        )

    def send_lift(k, _):
        lift_copy(lax.rem(me + k, n), me).start()
        return 0

    lax.fori_loop(1, n, send_lift, 0)

    load_acts.wait()
    dlow_query = (ADAPTER_SCALE * dlq_scr[...]).astype(BF16)

    def down(low, slot):
        return dot(low, acts_scr[:, pl.ds(pl.multiple_of(slot * wd, wd), wd)])

    def send_query(k, _):
        peer = lax.rem(me + k, n)
        send_d[peer, 0:half_rows, :] = down(dlow_query, peer).astype(BF16)
        query_copy(peer, me).start()
        return 0

    lax.fori_loop(1, n, send_query, 0)
    acc_d[0:half_rows, :] = down(dlow_query, me)

    ret.wait()
    dlow_value = (ADAPTER_SCALE * (dlv_scr[:, 0:tok] + ret_recv[...])).astype(BF16)

    def send_value(k, _):
        peer = lax.rem(me + k, n)
        send_d[peer, half_rows : 2 * half_rows, :] = down(dlow_value, peer).astype(BF16)
        value_copy(peer, me).start()
        return 0

    lax.fori_loop(1, n, send_value, 0)
    acc_d[half_rows : 2 * half_rows, :] = down(dlow_value, me)
    acc_l[...] = send_l[me].astype(F32)

    def gather(k, _):
        src = lax.rem(me + n - k, n)
        lift_copy(src, src).wait_recv()
        acc_l[...] += recv_l[src].astype(F32)
        query_copy(src, src).wait_recv()
        acc_d[0:half_rows, :] += recv_d[src, 0:half_rows, :].astype(F32)
        return 0

    lax.fori_loop(1, n, gather, 0)

    def gather_value(k, _):
        src = lax.rem(me + n - k, n)
        value_copy(src, src).wait_recv()
        acc_d[half_rows : 2 * half_rows, :] += recv_d[src, half_rows : 2 * half_rows, :].astype(F32)
        return 0

    lax.fori_loop(1, n, gather_value, 0)

    whole_d = acc_d[...]
    whole_l = acc_l[...]
    share_d[...] = whole_d.astype(BF16)
    share_l[...] = whole_l.astype(BF16)

    def to_dp(src, dst, ssem, rsem, peer, slot):
        return pltpu.make_async_remote_copy(
            src_ref=src,
            dst_ref=dst.at[slot],
            send_sem=ssem.at[peer],
            recv_sem=rsem.at[slot],
            device_id={"dp": peer},
            device_id_type=MESH,
        )

    def share_d_copy(peer, slot):
        return to_dp(share_d, peer_d, shd_ssem, shd_rsem, peer, slot)

    def share_l_copy(peer, slot):
        return to_dp(share_l, peer_l, shl_ssem, shl_rsem, peer, slot)

    def fac_copy(peer, slot):
        return to_dp(fac_send, fac_recv, fac_ssem, fac_rsem, peer, slot)

    def sq_copy(peer, slot):
        return to_seq(sq_send, sq_recv.at[slot], sq_ssem, sq_rsem, peer, slot)

    squares = jnp.sum(
        jnp.sum(whole_d * whole_d, 0, keepdims=True), 1, keepdims=True
    ) + jnp.sum(jnp.sum(whole_l * whole_l, 0, keepdims=True), 1, keepdims=True)
    sq_send[...] = jnp.broadcast_to(squares, sq_send.shape)

    def send_sq(k, _):
        sq_copy(lax.rem(me + k, n), me).start()
        return 0

    lax.fori_loop(1, n, send_sq, 0)
    for k in range(1, m):
        peer = lax.rem(ex + k, m)
        share_d_copy(peer, ex).start()
        share_l_copy(peer, ex).start()

    def gather_sq(k, total):
        src = lax.rem(me + n - k, n)
        sq_copy(src, src).wait_recv()
        return total + sq_recv[src]

    norm = jnp.sqrt(lax.fori_loop(1, n, gather_sq, sq_send[...]))
    norm_ref[...] = norm
    factor = math.sqrt(PCOUNT) / (norm + STABLE)
    fac_send[...] = factor
    for k in range(1, m):
        fac_copy(lax.rem(ex + k, m), ex).start()

    one = factor[0:1, 0:1]
    sum_d = whole_d * one
    sum_l = whole_l * one
    for k in range(1, m):
        src = lax.rem(ex + m - k, m)
        share_d_copy(src, src).wait_recv()
        share_l_copy(src, src).wait_recv()
        fac_copy(src, src).wait_recv()
        other = fac_recv[src][0:1, 0:1]
        sum_d = sum_d + peer_d[src].astype(F32) * other
        sum_l = sum_l + peer_l[src].astype(F32) * other
    oqd_ref[...] = sum_d[:half_rows] + NOISE_STD * nqd_ref[...]
    ovd_ref[...] = sum_d[half_rows:] + NOISE_STD * nvd_ref[...]
    oql_ref[...] = sum_l[:, 0:wq] + NOISE_STD * nql_ref[...]
    ovl_ref[...] = sum_l[:, wqp : wqp + wv] + NOISE_STD * nvl_ref[...]

    def finish(k, _):
        peer = lax.rem(me + k, n)
        lift_copy(peer, me).wait_send()
        query_copy(peer, me).wait_send()
        value_copy(peer, me).wait_send()
        sq_copy(peer, me).wait_send()
        return 0

    lax.fori_loop(1, n, finish, 0)
    for k in range(1, m):
        peer = lax.rem(ex + k, m)
        share_d_copy(peer, ex).wait_send()
        share_l_copy(peer, ex).wait_send()
        fac_copy(peer, ex).wait_send()


def body(
    n,
    m,
    activations,
    query_states,
    key_states,
    value_states,
    output_grad,
    query_lowrank,
    value_lowrank,
    query_up_matrix,
    value_up_matrix,
    noise_query_down,
    noise_query_lift,
    noise_value_down,
    noise_value_lift,
    block_order,
    valid_lengths,
):
    tok = query_states.shape[1]
    width = activations.shape[2]
    qw = query_states.shape[2]
    kvw = key_states.shape[2]
    rank = query_lowrank.shape[2]
    wd, wq, wv = width // n, qw // n, kvw // n
    wl = max(wq, HEAD) + HEAD
    half = HEAD // 2

    positions = block_order[0, 0] * tok + jnp.arange(tok, dtype=jnp.int32)
    freqs = ROPE_BASE ** (-2.0 * jnp.arange(half).astype(F32) / HEAD)
    freqs = jnp.concatenate([freqs, freqs])
    angle = positions.astype(F32)[:, None] * freqs[None, :]
    signs = jnp.where(jnp.arange(HEAD) < half, -1.0, 1.0).astype(F32)
    cosine = jnp.cos(angle)
    sine = signs[None, :] * jnp.sin(angle)

    vmem = pl.BlockSpec(memory_space=pltpu.VMEM)
    smem = pl.BlockSpec(memory_space=pltpu.SMEM)
    hbm = pl.BlockSpec(memory_space=pl.ANY)
    dma = pltpu.SemaphoreType.DMA
    norm, qd, ql, vd, vl = pl.pallas_call(
        functools.partial(kernel, n, m),
        out_shape=(
            jax.ShapeDtypeStruct((8, HEAD), F32),
            jax.ShapeDtypeStruct((rank, wd), F32),
            jax.ShapeDtypeStruct((rank, wq), F32),
            jax.ShapeDtypeStruct((rank, wd), F32),
            jax.ShapeDtypeStruct((rank, wv), F32),
        ),
        in_specs=[smem, smem, hbm, hbm, hbm] + [vmem] * 12,
        out_specs=(vmem,) * 5,
        scratch_shapes=[
            pltpu.VMEM((tok, qw), BF16),
            pltpu.VMEM((tok, qw), BF16),
            pltpu.VMEM((tok, width), BF16),
            pltpu.VMEM((2 * tok, kvw), BF16),
            pltpu.VMEM((2 * tok, kvw), BF16),
            pltpu.VMEM((rank, tok), BF16),
            pltpu.VMEM((kvw, 2 * tok), BF16),
            pltpu.VMEM((HEAD, tok), F32),
            pltpu.VMEM((HEAD, tok), F32),
            pltpu.VMEM((2 * tok, HEAD), F32),
            pltpu.VMEM((rank, tok), F32),
            pltpu.VMEM((rank, 2 * tok), F32),
            pltpu.VMEM((rank, tok), F32),
            pltpu.VMEM((rank, tok), F32),
            pltpu.VMEM((n, 2 * rank, wd), BF16),
            pltpu.VMEM((n, 2 * rank, wd), BF16),
            pltpu.VMEM((n, rank, wl), BF16),
            pltpu.VMEM((n, rank, wl), BF16),
            pltpu.VMEM((2 * rank, wd), F32),
            pltpu.VMEM((rank, wl), F32),
            pltpu.VMEM((2 * rank, wd), BF16),
            pltpu.VMEM((rank, wl), BF16),
            pltpu.VMEM((m, 2 * rank, wd), BF16),
            pltpu.VMEM((m, rank, wl), BF16),
            pltpu.VMEM((8, HEAD), F32),
            pltpu.VMEM((n, 8, HEAD), F32),
            pltpu.VMEM((8, HEAD), F32),
            pltpu.VMEM((m, 8, HEAD), F32),
            dma((3,)),
            dma((3,)),
            dma((3,)),
            dma,
            dma,
        ]
        + [dma((n,))] * 8
        + [dma((m,))] * 6,
        compiler_params=pltpu.CompilerParams(
            collective_id=0, has_side_effects=True, vmem_limit_bytes=48 * 1024 * 1024
        ),
        name="adapter_backward",
    )(
        block_order,
        valid_lengths,
        query_states[0],
        output_grad[0],
        activations[0],
        key_states[0],
        value_states[0],
        cosine,
        sine,
        query_lowrank[0].T,
        value_lowrank[0].T,
        query_up_matrix,
        value_up_matrix,
        noise_query_down.T,
        noise_query_lift,
        noise_value_down.T,
        noise_value_lift,
    )
    return (norm[0, 0:1], qd.T, ql, vd.T, vl)


def solution(mesh):
    in_specs = (
        P("dp", "seq", None),
        P("dp", "seq", None),
        P("dp", "seq", None),
        P("dp", "seq", None),
        P("dp", "seq", None),
        P("dp", "seq", None),
        P("dp", "seq", None),
        P(),
        P(),
        P("seq", None),
        P(None, "seq"),
        P("seq", None),
        P(None, "seq"),
        P("dp", "seq"),
        P("dp"),
    )
    out_specs = (P("dp"), P("seq", None), P(None, "seq"), P("seq", None), P(None, "seq"))
    inner = functools.partial(body, mesh.shape["seq"], mesh.shape["dp"])
    return jax.shard_map(inner, mesh=mesh, in_specs=in_specs, out_specs=out_specs, check_vma=False)
```

```python
import functools
import math

import jax
import jax.numpy as jnp
from jax import lax
from jax.experimental import pallas as pl
from jax.experimental.pallas import tpu as pltpu
from jax.sharding import PartitionSpec as P

HEAD = 128
PCOUNT = 335872
ADAPTER_SCALE = 2.0
NOISE_STD = 0.5
STABLE = 0.01
ROPE_BASE = 500000.0
NEG = -1e30
F32 = jnp.float32
BF16 = jnp.bfloat16
MESH = pl.DeviceIdType.MESH


def dot(a, b):
    return jnp.dot(a, b, preferred_element_type=F32)


def dot_nt(a, b):
    return lax.dot_general(a, b, (((1,), (1,)), ((), ())), preferred_element_type=F32)


def lane_piece(x, j, width):
    if width >= HEAD:
        return x
    if j:
        x = pltpu.roll(x, HEAD - j * width, 1)
    lanes = lax.broadcasted_iota(jnp.int32, x.shape, 1)
    return jnp.where(lanes < width, x, 0.0)


def kernel(
    n,
    m,
    order_ref,
    valid_ref,
    q_hbm,
    g_hbm,
    acts_hbm,
    k_hbm,
    v_hbm,
    cos_ref,
    sin_ref,
    qlt_hbm,
    vlt_hbm,
    qup_hbm,
    vup_hbm,
    nqd_hbm,
    nql_hbm,
    nvd_hbm,
    nvl_hbm,
    norm_ref,
    oqd_ref,
    oql_ref,
    ovd_ref,
    ovl_ref,
    q_scr,
    g_scr,
    acts_scr,
    k_ref,
    qlt_ref,
    vlt_ref,
    qup_ref,
    vup_ref,
    nqd_ref,
    nql_ref,
    nvd_ref,
    nvl_ref,
    kwin,
    vwin,
    vlt_prev,
    kt_scr,
    cost_scr,
    sint_scr,
    dv_scr,
    dlq_scr,
    dlv_scr,
    ret_send,
    ret_recv,
    pair_d,
    got_d,
    send_d,
    recv_d,
    send_l,
    got_l,
    pair_l,
    recv_l,
    acc_d,
    acc_l,
    share_d,
    share_l,
    peer_d,
    peer_l,
    sq_send,
    sq_recv,
    fac_send,
    fac_recv,
    local_sem,
    halo_ssem,
    halo_rsem,
    ret_ssem,
    ret_rsem,
    l1_ssem,
    l1_rsem,
    l2_ssem,
    l2_rsem,
    q1_ssem,
    q1_rsem,
    q2_ssem,
    q2_rsem,
    v1_ssem,
    v1_rsem,
    v2_ssem,
    v2_rsem,
    sq_ssem,
    sq_rsem,
    shd_ssem,
    shd_rsem,
    shl_ssem,
    shl_rsem,
    fac_ssem,
    fac_rsem,
):
    me = lax.axis_index("seq")
    ex = lax.axis_index("dp")
    side = lax.rem(me, 2)
    depth = me // 2
    nz = n // 2
    partner = me + 1 - 2 * side
    right = lax.rem(me + 1, n)
    left = lax.rem(me + n - 1, n)
    tok = k_ref.shape[0]
    groups = k_ref.shape[1] // HEAD
    heads = q_scr.shape[1] // (groups * HEAD)
    wd = acts_scr.shape[1] // n
    wq = q_scr.shape[1] // n
    wqp = max(wq, HEAD)
    wv = k_ref.shape[1] // n
    scaling = 1.0 / math.sqrt(HEAD)
    c2 = scaling * math.log2(math.e)

    def load(i, src, dst):
        copy = pltpu.make_async_copy(src, dst, local_sem.at[i])
        copy.start()
        return copy

    load_k = load(0, k_hbm, k_ref)
    load_q = load(3, q_hbm, q_scr)
    load_v = [
        load(4 + c, v_hbm.at[:, pl.ds(c * HEAD, HEAD)], vwin.at[c, pl.ds(0, tok)])
        for c in range(groups)
    ]
    load_g = load(8, g_hbm, g_scr)
    load_small = [
        load(9, qlt_hbm, qlt_ref),
        load(10, vlt_hbm, vlt_ref),
        load(11, qup_hbm, qup_ref),
        load(12, vup_hbm, vup_ref),
        load(13, nqd_hbm, nqd_ref),
        load(14, nql_hbm, nql_ref),
        load(15, nvd_hbm, nvd_ref),
        load(16, nvl_hbm, nvl_ref),
    ]
    load_acts = load(17, acts_hbm, acts_scr)

    barrier = pltpu.get_barrier_semaphore()

    def greet_seq(k, _):
        peer = lax.rem(me + k, n)
        pl.semaphore_signal(barrier, inc=1, device_id={"seq": peer}, device_id_type=MESH)
        return 0

    lax.fori_loop(1, n, greet_seq, 0)
    for k in range(1, m):
        peer = lax.rem(ex + k, m)
        pl.semaphore_signal(barrier, inc=1, device_id={"dp": peer}, device_id_type=MESH)

    load_k.wait()
    cos = cos_ref[...]
    sin = sin_ref[...]
    for c in range(groups):
        k = k_ref[:, c * HEAD : (c + 1) * HEAD].astype(F32)
        kr = k * cos + pltpu.roll(k, HEAD // 2, 1) * sin
        kwin[c, 0:tok, :] = kr.astype(BF16)
    pl.semaphore_wait(barrier, n - 1 + m - 1)

    def halo(i, src, dst):
        return pltpu.make_async_remote_copy(
            src_ref=src,
            dst_ref=dst,
            send_sem=halo_ssem.at[i],
            recv_sem=halo_rsem.at[i],
            device_id={"seq": right},
            device_id_type=MESH,
        )

    def key_halo(c):
        return halo(2 * c, kwin.at[c, pl.ds(0, tok)], kwin.at[c, pl.ds(tok, tok)])

    def value_halo(c):
        return halo(2 * c + 1, v_hbm.at[:, pl.ds(c * HEAD, HEAD)], vwin.at[c, pl.ds(tok, tok)])

    lowrank_halo = halo(2 * groups, vlt_hbm, vlt_prev)
    for c in range(groups):
        key_halo(c).start()
        value_halo(c).start()
        if c == 0:
            lowrank_halo.start()
    for c in range(groups):
        k = k_ref[:, c * HEAD : (c + 1) * HEAD].astype(F32)
        kr = k * cos + pltpu.roll(k, HEAD // 2, 1) * sin
        kt_scr[c, :, 0:tok] = kr.T.astype(BF16)
    cost_scr[...] = cos.T
    sint_scr[...] = sin.T
    send_l[...] = jnp.zeros_like(send_l)
    dlq_scr[...] = jnp.zeros_like(dlq_scr)
    dlv_scr[...] = jnp.zeros_like(dlv_scr)

    order = order_ref[0, 0]
    valid = valid_ref[0]
    rows = lax.broadcasted_iota(jnp.int32, (tok, HEAD), 0) + order * tok
    keep = jnp.where(rows < valid, 1.0, 0.0).astype(BF16)
    bias = jnp.where(order > 0, 0.0, NEG).astype(F32)

    load_q.wait()

    def rope_queries(h, _):
        cols = pl.ds(pl.multiple_of(h * HEAD, HEAD), HEAD)
        q = q_scr[:, cols].astype(F32)
        q_scr[:, cols] = (q * cos_ref[...] + pltpu.roll(q, HEAD // 2, 1) * sin_ref[...]).astype(BF16)
        return 0

    lax.fori_loop(0, groups * heads, rope_queries, 0, unroll=4)
    load_g.wait()
    for copy in load_v + load_small:
        copy.wait()
    lowrank_halo.wait()

    key_at = lax.broadcasted_iota(jnp.int32, (tok, tok), 0)
    row_at = lax.broadcasted_iota(jnp.int32, (tok, tok), 1)
    causal = key_at <= row_at

    def one_head(c, i):
        h = c * heads + i
        cols = pl.ds(pl.multiple_of(h * HEAD, HEAD), HEAD)
        qr = q_scr[:, cols]
        g = g_scr[:, cols] * keep
        s = dot_nt(kwin[c], qr)
        own = jnp.where(causal, s[:tok], NEG)
        prev = s[tok:]
        top = jnp.maximum(
            jnp.max(own, 0, keepdims=True), jnp.max(prev, 0, keepdims=True) + bias
        )
        shift = top * c2
        e_own = jnp.exp2(own * c2 - shift)
        e_prev = jnp.exp2(prev * c2 - (shift - bias))
        total = jnp.sum(e_own, 0, keepdims=True) + jnp.sum(e_prev, 0, keepdims=True)
        e = jnp.concatenate([e_own, e_prev], 0)
        inverse = 1.0 / total
        dp = dot_nt(vwin[c], g)
        delta = jnp.sum(e * dp, 0, keepdims=True) * inverse
        p = e * inverse
        ds = (p * (dp - delta)).astype(BF16)
        dv = dot(p.astype(BF16), g)
        dq = dot(kt_scr[c], ds) * scaling
        half = HEAD // 2
        swapped = jnp.concatenate([dq[half:], dq[:half]], 0)
        dq_low = (dq * cost_scr[...] - swapped * sint_scr[...]).astype(BF16)
        lift = ADAPTER_SCALE * dot_nt(qlt_ref[...], dq_low)
        dlq = dot(qup_ref[:, cols], dq_low)
        if wq >= HEAD:
            slot = h * HEAD // wq
            at = pl.multiple_of(lax.rem(h * HEAD, wq), HEAD)
            send_l[slot, :, pl.ds(at, HEAD)] = lift.astype(BF16)
        else:
            per = HEAD // wq
            for j in range(per):
                send_l[h * per + j, :, 0:HEAD] = lane_piece(lift, j, wq).astype(BF16)
        return dv, dlq

    def to_seq(src, dst, ssem, rsem, peer):
        return pltpu.make_async_remote_copy(
            src_ref=src,
            dst_ref=dst,
            send_sem=ssem,
            recv_sem=rsem,
            device_id={"seq": peer},
            device_id_type=MESH,
        )

    def lift_pair(z):
        return to_seq(
            send_l.at[2 * z + 1 - side], got_l.at[z], l1_ssem.at[z], l1_rsem.at[z], partner
        )

    unroll = 8

    def one_group(c, _):
        dv_scr[...] = jnp.zeros_like(dv_scr)
        key_halo(c).wait()
        value_halo(c).wait()
        kt_scr[c, :, tok : 2 * tok] = kwin[c, tok : 2 * tok, :].astype(F32).T.astype(BF16)

        def some_heads(step, _):
            dvs = None
            dlqs = None
            for u in range(unroll):
                dv, dlq = one_head(c, step * unroll + u)
                dvs = dv if dvs is None else dvs + dv
                dlqs = dlq if dlqs is None else dlqs + dlq
            dv_scr[...] += dvs
            dlq_scr[...] += dlqs
            return 0

        lax.fori_loop(0, heads // unroll, some_heads, 0)
        kcols = pl.ds(pl.multiple_of(c * HEAD, HEAD), HEAD)
        dv_low = dv_scr[...].astype(BF16)
        vup = vup_ref[:, kcols]
        dlv_scr[...] += dot_nt(vup, dv_low)
        vlift = ADAPTER_SCALE * (dot(vlt_ref[...], dv_low[:tok]) + dot(vlt_prev[...], dv_low[tok:]))
        per = HEAD // wv
        for j in range(per):
            send_l[c * per + j, :, wqp : wqp + HEAD] = lane_piece(vlift, j, wv).astype(BF16)
        per = nz // groups
        for j in range(per):
            lift_pair(c * per + j).start()
        return 0

    lax.fori_loop(0, groups, one_group, 0)

    ret_send[...] = dlv_scr[:, tok : 2 * tok]
    ret = pltpu.make_async_remote_copy(
        src_ref=ret_send,
        dst_ref=ret_recv,
        send_sem=ret_ssem,
        recv_sem=ret_rsem,
        device_id={"seq": left},
        device_id_type=MESH,
    )
    ret.start()

    def lift_copy(z, at):
        return to_seq(
            pair_l.at[z], recv_l.at[at], l2_ssem.at[z], l2_rsem.at[at], 2 * z + side
        )

    half_rows = qlt_ref.shape[0]
    upper = pl.ds(0, half_rows)
    lower = pl.ds(half_rows, half_rows)

    def down_pair(part, ssem, rsem):
        return lambda z: to_seq(
            pair_d.at[z, part], got_d.at[z, part], ssem.at[z], rsem.at[z], partner
        )

    def down_copy(part, ssem, rsem):
        return lambda z, at: to_seq(
            send_d.at[z, part], recv_d.at[at, part], ssem.at[z], rsem.at[at], 2 * z + side
        )

    query_pair = down_pair(upper, q1_ssem, q1_rsem)
    value_pair = down_pair(lower, v1_ssem, v1_rsem)
    query_copy = down_copy(upper, q2_ssem, q2_rsem)
    value_copy = down_copy(lower, v2_ssem, v2_rsem)

    load_acts.wait()
    dlow_query = (ADAPTER_SCALE * dlq_scr[...]).astype(BF16)

    def down(low, slot):
        return dot(low, acts_scr[:, pl.ds(pl.multiple_of(slot * wd, wd), wd)])

    def pair_query(k, _):
        z = lax.rem(depth + k, nz)
        pair_d[z, 0:half_rows, :] = down(dlow_query, 2 * z + 1 - side).astype(BF16)
        query_pair(z).start()
        return 0

    lax.fori_loop(1, nz + 1, pair_query, 0)

    def send_lift(k, _):
        z = lax.rem(depth + k, nz)
        lift_pair(z).wait_recv()
        pair_l[z] = (send_l[2 * z + side].astype(F32) + got_l[z].astype(F32)).astype(BF16)
        lift_copy(z, depth).start()
        return 0

    lax.fori_loop(1, nz, send_lift, 0)
    lift_pair(depth).wait_recv()
    acc_l[...] = send_l[me].astype(F32) + got_l[depth].astype(F32)

    ret.wait()
    dlow_value = (ADAPTER_SCALE * (dlv_scr[:, 0:tok] + ret_recv[...])).astype(BF16)

    def pair_value(k, _):
        z = lax.rem(depth + k, nz)
        pair_d[z, half_rows : 2 * half_rows, :] = down(dlow_value, 2 * z + 1 - side).astype(BF16)
        value_pair(z).start()
        return 0

    lax.fori_loop(1, nz + 1, pair_value, 0)

    def send_query(k, _):
        z = lax.rem(depth + k, nz)
        own = down(dlow_query, 2 * z + side)
        query_pair(z).wait_recv()
        send_d[z, 0:half_rows, :] = (own + got_d[z, 0:half_rows, :].astype(F32)).astype(BF16)
        query_copy(z, depth).start()
        return 0

    lax.fori_loop(1, nz, send_query, 0)

    def send_value(k, _):
        z = lax.rem(depth + k, nz)
        own = down(dlow_value, 2 * z + side)
        value_pair(z).wait_recv()
        got = got_d[z, half_rows : 2 * half_rows, :].astype(F32)
        send_d[z, half_rows : 2 * half_rows, :] = (own + got).astype(BF16)
        value_copy(z, depth).start()
        return 0

    lax.fori_loop(1, nz, send_value, 0)
    acc_d[0:half_rows, :] = down(dlow_query, me)
    acc_d[half_rows : 2 * half_rows, :] = down(dlow_value, me)
    query_pair(depth).wait_recv()
    value_pair(depth).wait_recv()
    acc_d[...] += got_d[depth].astype(F32)

    def gather(k, _):
        z = lax.rem(depth + nz - k, nz)
        lift_copy(z, z).wait_recv()
        acc_l[...] += recv_l[z].astype(F32)
        query_copy(z, z).wait_recv()
        acc_d[0:half_rows, :] += recv_d[z, 0:half_rows, :].astype(F32)
        return 0

    lax.fori_loop(1, nz, gather, 0)

    def gather_value(k, _):
        z = lax.rem(depth + nz - k, nz)
        value_copy(z, z).wait_recv()
        acc_d[half_rows : 2 * half_rows, :] += recv_d[z, half_rows : 2 * half_rows, :].astype(F32)
        return 0

    lax.fori_loop(1, nz, gather_value, 0)

    whole_d = acc_d[...]
    whole_l = acc_l[...]
    share_d[...] = whole_d.astype(BF16)
    share_l[...] = whole_l.astype(BF16)

    def to_dp(src, dst, ssem, rsem, peer, slot):
        return pltpu.make_async_remote_copy(
            src_ref=src,
            dst_ref=dst.at[slot],
            send_sem=ssem.at[peer],
            recv_sem=rsem.at[slot],
            device_id={"dp": peer},
            device_id_type=MESH,
        )

    def share_d_copy(peer, slot):
        return to_dp(share_d, peer_d, shd_ssem, shd_rsem, peer, slot)

    def share_l_copy(peer, slot):
        return to_dp(share_l, peer_l, shl_ssem, shl_rsem, peer, slot)

    def fac_copy(peer, slot):
        return to_dp(fac_send, fac_recv, fac_ssem, fac_rsem, peer, slot)

    def sq_copy(peer, slot):
        return to_seq(sq_send, sq_recv.at[slot], sq_ssem.at[peer], sq_rsem.at[slot], peer)

    squares = jnp.sum(
        jnp.sum(whole_d * whole_d, 0, keepdims=True), 1, keepdims=True
    ) + jnp.sum(jnp.sum(whole_l * whole_l, 0, keepdims=True), 1, keepdims=True)
    sq_send[...] = jnp.broadcast_to(squares, sq_send.shape)

    def send_sq(k, _):
        sq_copy(lax.rem(me + k, n), me).start()
        return 0

    lax.fori_loop(1, n, send_sq, 0)
    for k in range(1, m):
        peer = lax.rem(ex + k, m)
        share_d_copy(peer, ex).start()
        share_l_copy(peer, ex).start()

    def gather_sq(k, total):
        src = lax.rem(me + n - k, n)
        sq_copy(src, src).wait_recv()
        return total + sq_recv[src]

    norm = jnp.sqrt(lax.fori_loop(1, n, gather_sq, sq_send[...]))
    norm_ref[...] = norm
    factor = math.sqrt(PCOUNT) / (norm + STABLE)
    fac_send[...] = factor
    for k in range(1, m):
        fac_copy(lax.rem(ex + k, m), ex).start()

    one = factor[0:1, 0:1]
    sum_d = whole_d * one
    sum_l = whole_l * one
    for k in range(1, m):
        src = lax.rem(ex + m - k, m)
        share_d_copy(src, src).wait_recv()
        share_l_copy(src, src).wait_recv()
        fac_copy(src, src).wait_recv()
        other = fac_recv[src][0:1, 0:1]
        sum_d = sum_d + peer_d[src].astype(F32) * other
        sum_l = sum_l + peer_l[src].astype(F32) * other
    oqd_ref[...] = sum_d[:half_rows] + NOISE_STD * nqd_ref[...]
    ovd_ref[...] = sum_d[half_rows:] + NOISE_STD * nvd_ref[...]
    oql_ref[...] = sum_l[:, 0:wq] + NOISE_STD * nql_ref[...]
    ovl_ref[...] = sum_l[:, wqp : wqp + wv] + NOISE_STD * nvl_ref[...]

    def finish_sq(k, _):
        sq_copy(lax.rem(me + k, n), me).wait_send()
        return 0

    lax.fori_loop(1, n, finish_sq, 0)

    def finish_pair(z, _):
        lift_pair(z).wait_send()
        query_pair(z).wait_send()
        value_pair(z).wait_send()
        return 0

    lax.fori_loop(0, nz, finish_pair, 0)

    def finish_copy(k, _):
        z = lax.rem(depth + k, nz)
        lift_copy(z, depth).wait_send()
        query_copy(z, depth).wait_send()
        value_copy(z, depth).wait_send()
        return 0

    lax.fori_loop(1, nz, finish_copy, 0)
    for k in range(1, m):
        peer = lax.rem(ex + k, m)
        share_d_copy(peer, ex).wait_send()
        share_l_copy(peer, ex).wait_send()
        fac_copy(peer, ex).wait_send()


def body(
    n,
    m,
    activations,
    query_states,
    key_states,
    value_states,
    output_grad,
    query_lowrank,
    value_lowrank,
    query_up_matrix,
    value_up_matrix,
    noise_query_down,
    noise_query_lift,
    noise_value_down,
    noise_value_lift,
    block_order,
    valid_lengths,
):
    tok = query_states.shape[1]
    width = activations.shape[2]
    qw = query_states.shape[2]
    kvw = key_states.shape[2]
    rank = query_lowrank.shape[2]
    wd, wq, wv = width // n, qw // n, kvw // n
    wl = max(wq, HEAD) + HEAD
    groups = kvw // HEAD
    nz = n // 2
    half = HEAD // 2

    positions = block_order[0, 0] * tok + jnp.arange(tok, dtype=jnp.int32)
    freqs = ROPE_BASE ** (-2.0 * jnp.arange(half).astype(F32) / HEAD)
    freqs = jnp.concatenate([freqs, freqs])
    angle = positions.astype(F32)[:, None] * freqs[None, :]
    signs = jnp.where(jnp.arange(HEAD) < half, -1.0, 1.0).astype(F32)
    cosine = jnp.cos(angle)
    sine = signs[None, :] * jnp.sin(angle)

    vmem = pl.BlockSpec(memory_space=pltpu.VMEM)
    smem = pl.BlockSpec(memory_space=pltpu.SMEM)
    hbm = pl.BlockSpec(memory_space=pltpu.HBM)
    dma = pltpu.SemaphoreType.DMA
    norm, qd, ql, vd, vl = pl.pallas_call(
        functools.partial(kernel, n, m),
        out_shape=(
            jax.ShapeDtypeStruct((8, HEAD), F32),
            jax.ShapeDtypeStruct((rank, wd), F32),
            jax.ShapeDtypeStruct((rank, wq), F32),
            jax.ShapeDtypeStruct((rank, wd), F32),
            jax.ShapeDtypeStruct((rank, wv), F32),
        ),
        in_specs=[smem, smem] + [hbm] * 5 + [vmem] * 2 + [hbm] * 8,
        out_specs=(vmem,) * 5,
        scratch_shapes=[
            pltpu.VMEM((tok, qw), BF16),
            pltpu.VMEM((tok, qw), BF16),
            pltpu.VMEM((tok, width), BF16),
            pltpu.VMEM((tok, kvw), BF16),
            pltpu.VMEM((rank, tok), BF16),
            pltpu.VMEM((rank, tok), BF16),
            pltpu.VMEM((rank, qw), BF16),
            pltpu.VMEM((rank, kvw), BF16),
            pltpu.VMEM((rank, wd), F32),
            pltpu.VMEM((rank, wq), F32),
            pltpu.VMEM((rank, wd), F32),
            pltpu.VMEM((rank, wv), F32),
            pltpu.VMEM((groups, 2 * tok, HEAD), BF16),
            pltpu.VMEM((groups, 2 * tok, HEAD), BF16),
            pltpu.VMEM((rank, tok), BF16),
            pltpu.VMEM((groups, HEAD, 2 * tok), BF16),
            pltpu.VMEM((HEAD, tok), F32),
            pltpu.VMEM((HEAD, tok), F32),
            pltpu.VMEM((2 * tok, HEAD), F32),
            pltpu.VMEM((rank, tok), F32),
            pltpu.VMEM((rank, 2 * tok), F32),
            pltpu.VMEM((rank, tok), F32),
            pltpu.VMEM((rank, tok), F32),
            pltpu.VMEM((nz, 2 * rank, wd), BF16),
            pltpu.VMEM((nz, 2 * rank, wd), BF16),
            pltpu.VMEM((nz, 2 * rank, wd), BF16),
            pltpu.VMEM((nz, 2 * rank, wd), BF16),
            pltpu.VMEM((n, rank, wl), BF16),
            pltpu.VMEM((nz, rank, wl), BF16),
            pltpu.VMEM((nz, rank, wl), BF16),
            pltpu.VMEM((nz, rank, wl), BF16),
            pltpu.VMEM((2 * rank, wd), F32),
            pltpu.VMEM((rank, wl), F32),
            pltpu.VMEM((2 * rank, wd), BF16),
            pltpu.VMEM((rank, wl), BF16),
            pltpu.VMEM((m, 2 * rank, wd), BF16),
            pltpu.VMEM((m, rank, wl), BF16),
            pltpu.VMEM((8, HEAD), F32),
            pltpu.VMEM((n, 8, HEAD), F32),
            pltpu.VMEM((8, HEAD), F32),
            pltpu.VMEM((m, 8, HEAD), F32),
            dma((18,)),
            dma((2 * groups + 1,)),
            dma((2 * groups + 1,)),
            dma,
            dma,
        ]
        + [dma((nz,))] * 12
        + [dma((n,))] * 2
        + [dma((m,))] * 6,
        compiler_params=pltpu.CompilerParams(
            collective_id=0, has_side_effects=True, vmem_limit_bytes=60 * 1024 * 1024
        ),
        name="adapter_backward",
    )(
        block_order,
        valid_lengths,
        query_states[0],
        output_grad[0],
        activations[0],
        key_states[0],
        value_states[0],
        cosine,
        sine,
        query_lowrank[0].T,
        value_lowrank[0].T,
        query_up_matrix,
        value_up_matrix,
        noise_query_down.T,
        noise_query_lift,
        noise_value_down.T,
        noise_value_lift,
    )
    return (norm[0, 0:1], qd.T, ql, vd.T, vl)


def solution(mesh):
    in_specs = (
        P("dp", "seq", None),
        P("dp", "seq", None),
        P("dp", "seq", None),
        P("dp", "seq", None),
        P("dp", "seq", None),
        P("dp", "seq", None),
        P("dp", "seq", None),
        P(),
        P(),
        P("seq", None),
        P(None, "seq"),
        P("seq", None),
        P(None, "seq"),
        P("dp", "seq"),
        P("dp"),
    )
    out_specs = (P("dp"), P("seq", None), P(None, "seq"), P("seq", None), P(None, "seq"))
    inner = functools.partial(body, mesh.shape["seq"], mesh.shape["dp"])
    return jax.shard_map(inner, mesh=mesh, in_specs=in_specs, out_specs=out_specs, check_vma=False)
```

```python
import functools
import math

import jax
import jax.numpy as jnp
from jax import lax
from jax.experimental import pallas as pl
from jax.experimental.pallas import tpu as pltpu
from jax.sharding import PartitionSpec as P

HEAD = 128
PCOUNT = 335872
ADAPTER_SCALE = 2.0
NOISE_STD = 0.5
STABLE = 0.01
ROPE_BASE = 500000.0
NEG = -1e30
F32 = jnp.float32
BF16 = jnp.bfloat16
MESH = pl.DeviceIdType.MESH


def dot(a, b):
    return jnp.dot(a, b, preferred_element_type=F32)


def dot_nt(a, b):
    return lax.dot_general(a, b, (((1,), (1,)), ((), ())), preferred_element_type=F32)


def lane_piece(x, j, width):
    if width >= HEAD:
        return x
    if j:
        x = pltpu.roll(x, HEAD - j * width, 1)
    lanes = lax.broadcasted_iota(jnp.int32, x.shape, 1)
    return jnp.where(lanes < width, x, 0.0)


def kernel(
    n,
    m,
    order_ref,
    valid_ref,
    q_hbm,
    g_hbm,
    acts_hbm,
    k_hbm,
    v_hbm,
    cos_ref,
    sin_ref,
    qlt_hbm,
    vlt_hbm,
    qup_hbm,
    vup_hbm,
    nqd_hbm,
    nql_hbm,
    nvd_hbm,
    nvl_hbm,
    out_ref,
    q_scr,
    g_scr,
    acts_scr,
    k_ref,
    qlt_ref,
    vlt_ref,
    qup_ref,
    vup_ref,
    nqd_ref,
    nql_ref,
    nvd_ref,
    nvl_ref,
    kwin,
    vwin,
    vlt_prev,
    kt_scr,
    cost_scr,
    sint_scr,
    dlq_scr,
    dlv_scr,
    ret_send,
    ret_recv,
    pair_d,
    got_d,
    send_d,
    recv_d,
    send_l,
    got_l,
    pair_l,
    recv_l,
    acc_d,
    acc_l,
    share_d,
    share_l,
    peer_d,
    peer_l,
    sq_send,
    sq_recv,
    fac_send,
    fac_recv,
    local_sem,
    halo_ssem,
    halo_rsem,
    ret_ssem,
    ret_rsem,
    l1_ssem,
    l1_rsem,
    l2_ssem,
    l2_rsem,
    q1_ssem,
    q1_rsem,
    q2_ssem,
    q2_rsem,
    v1_ssem,
    v1_rsem,
    v2_ssem,
    v2_rsem,
    sq_ssem,
    sq_rsem,
    shd_ssem,
    shd_rsem,
    shl_ssem,
    shl_rsem,
    fac_ssem,
    fac_rsem,
):
    me = lax.axis_index("seq")
    ex = lax.axis_index("dp")
    side = lax.rem(me, 2)
    depth = me // 2
    nz = n // 2
    partner = me + 1 - 2 * side
    right = lax.rem(me + 1, n)
    left = lax.rem(me + n - 1, n)
    tok = k_ref.shape[0]
    groups = k_ref.shape[1] // HEAD
    heads = q_scr.shape[1] // (groups * HEAD)
    wd = acts_scr.shape[1] // n
    wq = q_scr.shape[1] // n
    wqp = max(wq, HEAD)
    wv = k_ref.shape[1] // n
    scaling = 1.0 / math.sqrt(HEAD)
    c2 = scaling * math.log2(math.e)

    def load(i, src, dst):
        copy = pltpu.make_async_copy(src, dst, local_sem.at[i])
        copy.start()
        return copy

    load_k = load(0, k_hbm, k_ref)
    load_q = load(3, q_hbm, q_scr)
    load_v = [
        load(4 + c, v_hbm.at[:, pl.ds(c * HEAD, HEAD)], vwin.at[c, pl.ds(0, tok)])
        for c in range(groups)
    ]
    load_g = load(8, g_hbm, g_scr)
    load_small = [
        load(9, qlt_hbm, qlt_ref),
        load(10, vlt_hbm, vlt_ref),
        load(11, qup_hbm, qup_ref),
        load(12, vup_hbm, vup_ref),
        load(13, nqd_hbm, nqd_ref),
        load(14, nql_hbm, nql_ref),
        load(15, nvd_hbm, nvd_ref),
        load(16, nvl_hbm, nvl_ref),
    ]
    load_acts = load(17, acts_hbm, acts_scr)

    barrier = pltpu.get_barrier_semaphore()

    def greet_seq(k, _):
        peer = lax.rem(me + k, n)
        pl.semaphore_signal(barrier, inc=1, device_id={"seq": peer}, device_id_type=MESH)
        return 0

    lax.fori_loop(1, n, greet_seq, 0)
    for k in range(1, m):
        peer = lax.rem(ex + k, m)
        pl.semaphore_signal(barrier, inc=1, device_id={"dp": peer}, device_id_type=MESH)

    load_k.wait()
    cos = cos_ref[...]
    sin = sin_ref[...]
    for c in range(groups):
        k = k_ref[:, c * HEAD : (c + 1) * HEAD].astype(F32)
        kr = k * cos + pltpu.roll(k, HEAD // 2, 1) * sin
        kwin[c, 0:tok, :] = kr.astype(BF16)
    pl.semaphore_wait(barrier, n - 1 + m - 1)

    def halo(i, src, dst):
        return pltpu.make_async_remote_copy(
            src_ref=src,
            dst_ref=dst,
            send_sem=halo_ssem.at[i],
            recv_sem=halo_rsem.at[i],
            device_id={"seq": right},
            device_id_type=MESH,
        )

    def key_halo(c):
        return halo(2 * c, kwin.at[c, pl.ds(0, tok)], kwin.at[c, pl.ds(tok, tok)])

    def value_halo(c):
        return halo(2 * c + 1, v_hbm.at[:, pl.ds(c * HEAD, HEAD)], vwin.at[c, pl.ds(tok, tok)])

    lowrank_halo = halo(2 * groups, vlt_hbm, vlt_prev)
    for c in range(groups):
        key_halo(c).start()
        value_halo(c).start()
        if c == 0:
            lowrank_halo.start()
    for c in range(groups):
        k = k_ref[:, c * HEAD : (c + 1) * HEAD].astype(F32)
        kr = k * cos + pltpu.roll(k, HEAD // 2, 1) * sin
        kt_scr[c, :, 0:tok] = kr.T.astype(BF16)
    cost_scr[...] = cos.T
    sint_scr[...] = sin.T
    send_l[...] = jnp.zeros_like(send_l)
    dlq_scr[...] = jnp.zeros_like(dlq_scr)
    dlv_scr[...] = jnp.zeros_like(dlv_scr)

    order = order_ref[0, 0]
    valid = valid_ref[0]
    rows = lax.broadcasted_iota(jnp.int32, (tok, HEAD), 0) + order * tok
    keep = jnp.where(rows < valid, 1.0, 0.0).astype(BF16)
    bias = jnp.where(order > 0, 0.0, NEG).astype(F32)

    load_q.wait()

    def rope_queries(h, _):
        cols = pl.ds(pl.multiple_of(h * HEAD, HEAD), HEAD)
        q = q_scr[:, cols].astype(F32)
        q_scr[:, cols] = (q * cos_ref[...] + pltpu.roll(q, HEAD // 2, 1) * sin_ref[...]).astype(BF16)
        return 0

    lax.fori_loop(0, groups * heads, rope_queries, 0, unroll=4)
    load_g.wait()
    for copy in load_v + load_small:
        copy.wait()
    lowrank_halo.wait()

    key_at = lax.broadcasted_iota(jnp.int32, (tok, tok), 0)
    row_at = lax.broadcasted_iota(jnp.int32, (tok, tok), 1)
    causal = key_at <= row_at

    def one_head(c, i):
        h = c * heads + i
        cols = pl.ds(pl.multiple_of(h * HEAD, HEAD), HEAD)
        qr = q_scr[:, cols]
        g = g_scr[:, cols] * keep
        s = dot_nt(kwin[c], qr)
        dp = dot_nt(vwin[c], g)
        mid = tok // 2

        def right_half(row, op, extra):
            return jnp.concatenate([row[:, :mid], op(row[:, mid:], extra)], 1)

        def key_max(x):
            return jnp.max(x, 0, keepdims=True)

        def key_sum(x):
            return jnp.sum(x, 0, keepdims=True)

        first = jnp.where(causal[:mid], s[:mid], NEG)
        second = jnp.where(causal[:mid, :mid], s[mid:tok, mid:], NEG)
        prev = s[tok:]
        top = jnp.maximum(key_max(first), key_max(prev) + bias)
        top = right_half(top, jnp.maximum, key_max(second))
        shift = top * c2
        e1 = jnp.exp2(first * c2 - shift)
        e2 = jnp.exp2(second * c2 - shift[:, mid:])
        e3 = jnp.exp2(prev * c2 - (shift - bias))
        total = right_half(key_sum(e1) + key_sum(e3), jnp.add, key_sum(e2))
        inverse = 1.0 / total
        dp1, dp2, dp3 = dp[:mid], dp[mid:tok, mid:], dp[tok:]
        delta = right_half(key_sum(e1 * dp1) + key_sum(e3 * dp3), jnp.add, key_sum(e2 * dp2))
        delta = delta * inverse
        p1, p2, p3 = e1 * inverse, e2 * inverse[:, mid:], e3 * inverse
        none = jnp.zeros((tok - mid, mid), BF16)

        def window(x1, x2, x3):
            low = jnp.concatenate([none, x2.astype(BF16)], 1)
            return jnp.concatenate([x1.astype(BF16), low, x3.astype(BF16)], 0)

        p = window(p1, p2, p3)
        ds = window(p1 * (dp1 - delta), p2 * (dp2 - delta[:, mid:]), p3 * (dp3 - delta))
        dq = dot(kt_scr[c], ds) * scaling
        half = HEAD // 2
        swapped = jnp.concatenate([dq[half:], dq[:half]], 0)
        dq_low = (dq * cost_scr[...] - swapped * sint_scr[...]).astype(BF16)
        return p, g, dq_low

    def write_lift(h, lift):
        if wq >= HEAD:
            slot = h * HEAD // wq
            at = pl.multiple_of(lax.rem(h * HEAD, wq), HEAD)
            send_l[slot, :, pl.ds(at, HEAD)] = lift.astype(BF16)
        else:
            per = HEAD // wq
            for j in range(per):
                send_l[h * per + j, :, 0:HEAD] = lane_piece(lift, j, wq).astype(BF16)

    def to_seq(src, dst, ssem, rsem, peer):
        return pltpu.make_async_remote_copy(
            src_ref=src,
            dst_ref=dst,
            send_sem=ssem,
            recv_sem=rsem,
            device_id={"seq": peer},
            device_id_type=MESH,
        )

    def lift_pair(z):
        return to_seq(
            send_l.at[2 * z + 1 - side], got_l.at[z], l1_ssem.at[z], l1_rsem.at[z], partner
        )

    def one_group(c, _):
        key_halo(c).wait()
        value_halo(c).wait()
        kt_scr[c, :, tok : 2 * tok] = kwin[c, tok : 2 * tok, :].astype(F32).T.astype(BF16)

        parts = [one_head(c, i) for i in range(heads)]
        probs = jnp.concatenate([part[0] for part in parts], 1)
        grads = jnp.concatenate([part[1] for part in parts], 0)
        turned = jnp.concatenate([part[2] for part in parts], 0)
        dv_low = dot(probs, grads).astype(BF16)
        span = heads * HEAD
        dlq_scr[...] += dot(qup_ref[:, pl.ds(pl.multiple_of(c * span, span), span)], turned)
        lifts = ADAPTER_SCALE * dot_nt(qlt_ref[...], turned)
        for i in range(heads):
            write_lift(c * heads + i, lifts[:, i * HEAD : (i + 1) * HEAD])
        kcols = pl.ds(pl.multiple_of(c * HEAD, HEAD), HEAD)
        vup = vup_ref[:, kcols]
        dlv_scr[...] += dot_nt(vup, dv_low)
        vlift = ADAPTER_SCALE * (dot(vlt_ref[...], dv_low[:tok]) + dot(vlt_prev[...], dv_low[tok:]))
        per = HEAD // wv
        for j in range(per):
            send_l[c * per + j, :, wqp : wqp + HEAD] = lane_piece(vlift, j, wv).astype(BF16)
        per = nz // groups
        for j in range(per):
            lift_pair(c * per + j).start()
        return 0

    lax.fori_loop(0, groups, one_group, 0)

    ret_send[...] = dlv_scr[:, tok : 2 * tok]
    ret = pltpu.make_async_remote_copy(
        src_ref=ret_send,
        dst_ref=ret_recv,
        send_sem=ret_ssem,
        recv_sem=ret_rsem,
        device_id={"seq": left},
        device_id_type=MESH,
    )
    ret.start()

    def lift_copy(z, at):
        return to_seq(
            pair_l.at[z], recv_l.at[at], l2_ssem.at[z], l2_rsem.at[at], 2 * z + side
        )

    half_rows = qlt_ref.shape[0]
    upper = pl.ds(0, half_rows)
    lower = pl.ds(half_rows, half_rows)

    def down_pair(part, ssem, rsem):
        return lambda z: to_seq(
            pair_d.at[z, part], got_d.at[z, part], ssem.at[z], rsem.at[z], partner
        )

    def down_copy(part, ssem, rsem):
        return lambda z, at: to_seq(
            send_d.at[z, part], recv_d.at[at, part], ssem.at[z], rsem.at[at], 2 * z + side
        )

    query_pair = down_pair(upper, q1_ssem, q1_rsem)
    value_pair = down_pair(lower, v1_ssem, v1_rsem)
    query_copy = down_copy(upper, q2_ssem, q2_rsem)
    value_copy = down_copy(lower, v2_ssem, v2_rsem)

    load_acts.wait()
    dlow_query = (ADAPTER_SCALE * dlq_scr[...]).astype(BF16)

    def down(low, slot):
        return dot(low, acts_scr[:, pl.ds(pl.multiple_of(slot * wd, wd), wd)])

    def pair_query(k, _):
        z = lax.rem(depth + k, nz)
        pair_d[z, 0:half_rows, :] = down(dlow_query, 2 * z + 1 - side).astype(BF16)
        query_pair(z).start()
        return 0

    lax.fori_loop(1, nz + 1, pair_query, 0)

    def send_lift(k, _):
        z = lax.rem(depth + k, nz)
        lift_pair(z).wait_recv()
        pair_l[z] = (send_l[2 * z + side].astype(F32) + got_l[z].astype(F32)).astype(BF16)
        lift_copy(z, depth).start()
        return 0

    lax.fori_loop(1, nz, send_lift, 0)
    lift_pair(depth).wait_recv()
    acc_l[...] = send_l[me].astype(F32) + got_l[depth].astype(F32)

    ret.wait()
    dlow_value = (ADAPTER_SCALE * (dlv_scr[:, 0:tok] + ret_recv[...])).astype(BF16)

    def pair_value(k, _):
        z = lax.rem(depth + k, nz)
        pair_d[z, half_rows : 2 * half_rows, :] = down(dlow_value, 2 * z + 1 - side).astype(BF16)
        value_pair(z).start()
        return 0

    lax.fori_loop(1, nz + 1, pair_value, 0)

    def send_query(k, _):
        z = lax.rem(depth + k, nz)
        own = down(dlow_query, 2 * z + side)
        query_pair(z).wait_recv()
        send_d[z, 0:half_rows, :] = (own + got_d[z, 0:half_rows, :].astype(F32)).astype(BF16)
        query_copy(z, depth).start()
        return 0

    lax.fori_loop(1, nz, send_query, 0)

    def send_value(k, _):
        z = lax.rem(depth + k, nz)
        own = down(dlow_value, 2 * z + side)
        value_pair(z).wait_recv()
        got = got_d[z, half_rows : 2 * half_rows, :].astype(F32)
        send_d[z, half_rows : 2 * half_rows, :] = (own + got).astype(BF16)
        value_copy(z, depth).start()
        return 0

    lax.fori_loop(1, nz, send_value, 0)
    acc_d[0:half_rows, :] = down(dlow_query, me)
    acc_d[half_rows : 2 * half_rows, :] = down(dlow_value, me)
    query_pair(depth).wait_recv()
    value_pair(depth).wait_recv()
    acc_d[...] += got_d[depth].astype(F32)

    def gather(k, _):
        z = lax.rem(depth + nz - k, nz)
        lift_copy(z, z).wait_recv()
        acc_l[...] += recv_l[z].astype(F32)
        query_copy(z, z).wait_recv()
        acc_d[0:half_rows, :] += recv_d[z, 0:half_rows, :].astype(F32)
        return 0

    lax.fori_loop(1, nz, gather, 0)

    def gather_value(k, _):
        z = lax.rem(depth + nz - k, nz)
        value_copy(z, z).wait_recv()
        acc_d[half_rows : 2 * half_rows, :] += recv_d[z, half_rows : 2 * half_rows, :].astype(F32)
        return 0

    lax.fori_loop(1, nz, gather_value, 0)

    whole_d = acc_d[...]
    whole_l = acc_l[...]
    share_d[...] = whole_d.astype(BF16)
    share_l[...] = whole_l.astype(BF16)

    def to_dp(src, dst, ssem, rsem, peer, slot):
        return pltpu.make_async_remote_copy(
            src_ref=src,
            dst_ref=dst.at[slot],
            send_sem=ssem.at[peer],
            recv_sem=rsem.at[slot],
            device_id={"dp": peer},
            device_id_type=MESH,
        )

    def share_d_copy(peer, slot):
        return to_dp(share_d, peer_d, shd_ssem, shd_rsem, peer, slot)

    def share_l_copy(peer, slot):
        return to_dp(share_l, peer_l, shl_ssem, shl_rsem, peer, slot)

    def fac_copy(peer, slot):
        return to_dp(fac_send, fac_recv, fac_ssem, fac_rsem, peer, slot)

    def sq_copy(peer, slot):
        return to_seq(sq_send, sq_recv.at[slot], sq_ssem.at[peer], sq_rsem.at[slot], peer)

    squares = jnp.sum(
        jnp.sum(whole_d * whole_d, 0, keepdims=True), 1, keepdims=True
    ) + jnp.sum(jnp.sum(whole_l * whole_l, 0, keepdims=True), 1, keepdims=True)
    sq_send[...] = jnp.broadcast_to(squares, sq_send.shape)

    def send_sq(k, _):
        sq_copy(lax.rem(me + k, n), me).start()
        return 0

    lax.fori_loop(1, n, send_sq, 0)
    for k in range(1, m):
        peer = lax.rem(ex + k, m)
        share_d_copy(peer, ex).start()
        share_l_copy(peer, ex).start()

    def gather_sq(k, total):
        src = lax.rem(me + n - k, n)
        sq_copy(src, src).wait_recv()
        return total + sq_recv[src]

    norm = jnp.sqrt(lax.fori_loop(1, n, gather_sq, sq_send[...]))
    factor = math.sqrt(PCOUNT) / (norm + STABLE)
    fac_send[...] = factor
    for k in range(1, m):
        fac_copy(lax.rem(ex + k, m), ex).start()

    one = factor[0:1, 0:1]
    sum_d = whole_d * one
    sum_l = whole_l * one
    for k in range(1, m):
        src = lax.rem(ex + m - k, m)
        share_d_copy(src, src).wait_recv()
        share_l_copy(src, src).wait_recv()
        fac_copy(src, src).wait_recv()
        other = fac_recv[src][0:1, 0:1]
        sum_d = sum_d + peer_d[src].astype(F32) * other
        sum_l = sum_l + peer_l[src].astype(F32) * other
    rank = half_rows
    out_ref[0:rank, 0:wd] = sum_d[:rank] + NOISE_STD * nqd_ref[...]
    out_ref[rank : 2 * rank, 0:wd] = sum_d[rank:] + NOISE_STD * nvd_ref[...]
    out_ref[2 * rank : 3 * rank, 0:wq] = sum_l[:, 0:wq] + NOISE_STD * nql_ref[...]
    out_ref[2 * rank : 3 * rank, wqp : wqp + wv] = (
        sum_l[:, wqp : wqp + wv] + NOISE_STD * nvl_ref[...]
    )
    out_ref[3 * rank : 3 * rank + 8, 0:HEAD] = norm

    def finish_sq(k, _):
        sq_copy(lax.rem(me + k, n), me).wait_send()
        return 0

    lax.fori_loop(1, n, finish_sq, 0)

    def finish_pair(z, _):
        lift_pair(z).wait_send()
        query_pair(z).wait_send()
        value_pair(z).wait_send()
        return 0

    lax.fori_loop(0, nz, finish_pair, 0)

    def finish_copy(k, _):
        z = lax.rem(depth + k, nz)
        lift_copy(z, depth).wait_send()
        query_copy(z, depth).wait_send()
        value_copy(z, depth).wait_send()
        return 0

    lax.fori_loop(1, nz, finish_copy, 0)
    for k in range(1, m):
        peer = lax.rem(ex + k, m)
        share_d_copy(peer, ex).wait_send()
        share_l_copy(peer, ex).wait_send()
        fac_copy(peer, ex).wait_send()


def deliver(packed, out_norm, out_qd, out_ql, out_vd, out_vl):
    rank, wd = out_qd.shape
    wq = out_ql.shape[1]
    at = max(wq, HEAD)
    out_norm[0] = packed[3 * rank, 0]
    out_qd[...] = packed[0:rank, 0:wd]
    out_vd[...] = packed[rank : 2 * rank, 0:wd]
    out_ql[...] = packed[2 * rank : 3 * rank, 0:wq]
    out_vl[...] = packed[2 * rank : 3 * rank, at : at + out_vl.shape[1]]


def body(
    n,
    m,
    activations,
    query_states,
    key_states,
    value_states,
    output_grad,
    query_lowrank,
    value_lowrank,
    query_up_matrix,
    value_up_matrix,
    noise_query_down,
    noise_query_lift,
    noise_value_down,
    noise_value_lift,
    block_order,
    valid_lengths,
):
    tok = query_states.shape[1]
    width = activations.shape[2]
    qw = query_states.shape[2]
    kvw = key_states.shape[2]
    rank = query_lowrank.shape[2]
    wd, wq, wv = width // n, qw // n, kvw // n
    wl = max(wq, HEAD) + HEAD
    groups = kvw // HEAD
    nz = n // 2
    half = HEAD // 2

    positions = block_order[0, 0] * tok + jnp.arange(tok, dtype=jnp.int32)
    freqs = ROPE_BASE ** (-2.0 * jnp.arange(half).astype(F32) / HEAD)
    freqs = jnp.concatenate([freqs, freqs])
    angle = positions.astype(F32)[:, None] * freqs[None, :]
    signs = jnp.where(jnp.arange(HEAD) < half, -1.0, 1.0).astype(F32)
    cosine = jnp.cos(angle)
    sine = signs[None, :] * jnp.sin(angle)

    vmem = pl.BlockSpec(memory_space=pltpu.VMEM)
    smem = pl.BlockSpec(memory_space=pltpu.SMEM)
    hbm = pl.BlockSpec(memory_space=pltpu.HBM)
    dma = pltpu.SemaphoreType.DMA
    packed = pl.pallas_call(
        functools.partial(kernel, n, m),
        out_shape=jax.ShapeDtypeStruct((3 * rank + 8, max(wd, wl)), F32),
        in_specs=[smem, smem] + [hbm] * 5 + [vmem] * 2 + [hbm] * 8,
        out_specs=vmem,
        scratch_shapes=[
            pltpu.VMEM((tok, qw), BF16),
            pltpu.VMEM((tok, qw), BF16),
            pltpu.VMEM((tok, width), BF16),
            pltpu.VMEM((tok, kvw), BF16),
            pltpu.VMEM((rank, tok), BF16),
            pltpu.VMEM((rank, tok), BF16),
            pltpu.VMEM((rank, qw), BF16),
            pltpu.VMEM((rank, kvw), BF16),
            pltpu.VMEM((rank, wd), F32),
            pltpu.VMEM((rank, wq), F32),
            pltpu.VMEM((rank, wd), F32),
            pltpu.VMEM((rank, wv), F32),
            pltpu.VMEM((groups, 2 * tok, HEAD), BF16),
            pltpu.VMEM((groups, 2 * tok, HEAD), BF16),
            pltpu.VMEM((rank, tok), BF16),
            pltpu.VMEM((groups, HEAD, 2 * tok), BF16),
            pltpu.VMEM((HEAD, tok), F32),
            pltpu.VMEM((HEAD, tok), F32),
            pltpu.VMEM((rank, tok), F32),
            pltpu.VMEM((rank, 2 * tok), F32),
            pltpu.VMEM((rank, tok), F32),
            pltpu.VMEM((rank, tok), F32),
            pltpu.VMEM((nz, 2 * rank, wd), BF16),
            pltpu.VMEM((nz, 2 * rank, wd), BF16),
            pltpu.VMEM((nz, 2 * rank, wd), BF16),
            pltpu.VMEM((nz, 2 * rank, wd), BF16),
            pltpu.VMEM((n, rank, wl), BF16),
            pltpu.VMEM((nz, rank, wl), BF16),
            pltpu.VMEM((nz, rank, wl), BF16),
            pltpu.VMEM((nz, rank, wl), BF16),
            pltpu.VMEM((2 * rank, wd), F32),
            pltpu.VMEM((rank, wl), F32),
            pltpu.VMEM((2 * rank, wd), BF16),
            pltpu.VMEM((rank, wl), BF16),
            pltpu.VMEM((m, 2 * rank, wd), BF16),
            pltpu.VMEM((m, rank, wl), BF16),
            pltpu.VMEM((8, HEAD), F32),
            pltpu.VMEM((n, 8, HEAD), F32),
            pltpu.VMEM((8, HEAD), F32),
            pltpu.VMEM((m, 8, HEAD), F32),
            dma((18,)),
            dma((2 * groups + 1,)),
            dma((2 * groups + 1,)),
            dma,
            dma,
        ]
        + [dma((nz,))] * 12
        + [dma((n,))] * 2
        + [dma((m,))] * 6,
        compiler_params=pltpu.CompilerParams(
            collective_id=0, has_side_effects=True, vmem_limit_bytes=60 * 1024 * 1024
        ),
        name="adapter_backward",
    )(
        block_order,
        valid_lengths,
        query_states[0],
        output_grad[0],
        activations[0],
        key_states[0],
        value_states[0],
        cosine,
        sine,
        query_lowrank[0].T,
        value_lowrank[0].T,
        query_up_matrix,
        value_up_matrix,
        noise_query_down.T,
        noise_query_lift,
        noise_value_down.T,
        noise_value_lift,
    )
    norm, qd, ql, vd, vl = pl.pallas_call(
        deliver,
        out_shape=(
            jax.ShapeDtypeStruct((1,), F32),
            jax.ShapeDtypeStruct((rank, wd), F32),
            jax.ShapeDtypeStruct((rank, wq), F32),
            jax.ShapeDtypeStruct((rank, wd), F32),
            jax.ShapeDtypeStruct((rank, wv), F32),
        ),
        in_specs=[vmem],
        out_specs=(smem,) + (vmem,) * 4,
        name="deliver",
    )(packed)
    return (norm, qd.T, ql, vd.T, vl)


def solution(mesh):
    in_specs = (
        P("dp", "seq", None),
        P("dp", "seq", None),
        P("dp", "seq", None),
        P("dp", "seq", None),
        P("dp", "seq", None),
        P("dp", "seq", None),
        P("dp", "seq", None),
        P(),
        P(),
        P("seq", None),
        P(None, "seq"),
        P("seq", None),
        P(None, "seq"),
        P("dp", "seq"),
        P("dp"),
    )
    out_specs = (P("dp"), P("seq", None), P(None, "seq"), P("seq", None), P(None, "seq"))
    inner = functools.partial(body, mesh.shape["seq"], mesh.shape["dp"])
    return jax.shard_map(inner, mesh=mesh, in_specs=in_specs, out_specs=out_specs, check_vma=False)
```
